128 devices in a mesh: tensor: 8 (over x, z_lo), seq: 16 (over y, z_hi, core).
Axes of the slice: x: 4, y: 4, z: 4 (z_hi: 2, z_lo: 2; z = z_hi * 2 + z_lo), core: 2. Of those that a mesh axis runs over, the one named last changes fastest.
Arguments:
- context: bfloat16 [2048, 18432], P('seq', 'tensor'), may hold values from -6 to 6
- out_proj: bfloat16 [18432, 18432], P('tensor', 'seq'), may hold values from -0.046875 to 0.046875
- student: bfloat16 [2048, 6144], P('seq', 'tensor'), may hold values from -6 to 6
- student_map: bfloat16 [6144, 18432], P('tensor', 'seq'), may hold values from -0.078125 to 0.078125
Outputs:
- grad_map: float32 [6144, 18432], P('tensor', 'seq')
- grad_student: float32 [2048, 6144], P('seq', 'tensor')
The draws below stay inside these ranges and needn't reach their ends.
All inputs are finite; a program needn't handle non-finite values.
Results may differ from the reference program's by a relative error of at most 0.0027.
Values may be sent and summed in bfloat16 or wider, within the bound.
No kernel may reach another device: no remote copies, remote signals or barrier semaphores. Data moves between devices by JAX's collectives and lax.ppermute only.
A program may use at most 128 MiB of HBM per device.

```python
import jax
import jax.numpy as jnp

D = 18432
DS = 6144
HD = 18432
TOKENS = 2048


def block_levels(own_key, shape, cuts, low, top_value):
    gain, own = 1.0, jax.random.fold_in(own_key, 6)
    for position, blocks in cuts:
        steps = jnp.exp(jax.random.uniform(jax.random.fold_in(own, position), (blocks,), jnp.float32, low / len(cuts), top_value / len(cuts)))
        gain = gain * jnp.repeat(steps, shape[position] // blocks).reshape([-1 if axis == position else 1 for axis in range(len(shape))])
    return gain


def gaussian(key, dims, spread, reach, cuts=(), held_as=jnp.bfloat16):
    array = jax.random.normal(key, dims, jnp.float32) * spread
    if len(cuts) > 0:
        array = block_levels(key, dims, cuts, -0.22, 0.18) * array
    return jnp.clip(array, min=-reach, max=reach).astype(held_as)


def setup_inputs(seed: int = 0) -> dict:
    arg_keys = jax.random.split(jax.random.key(seed), 5)
    return {
        "context": gaussian(arg_keys[0], (TOKENS, HD), 1.0, 6.0, ((0, 16), (1, 8))),
        "out_proj": gaussian(arg_keys[1], (HD, D), HD ** -0.5, 0.046875, ((0, 8), (1, 16))),
        "student": gaussian(arg_keys[2], (TOKENS, DS), 1.0, 6.0, ((0, 16), (1, 8))),
        "student_map": gaussian(arg_keys[3], (DS, D), DS ** -0.5, 0.078125, ((0, 8), (1, 16))),
    }


def reference(context, out_proj, student, student_map):
    teacher = jnp.dot(context, out_proj, preferred_element_type=jnp.float32)
    mapped = jnp.dot(student, student_map, preferred_element_type=jnp.float32)
    residual = (mapped - teacher).astype(jnp.bfloat16)
    grad_map = jnp.dot(student.T, residual, preferred_element_type=jnp.float32) / TOKENS
    grad_student = jnp.dot(residual, student_map.T, preferred_element_type=jnp.float32)
    return grad_map, grad_student
```

```python
import jax
import jax.numpy as jnp
from jax import lax
from jax.sharding import PartitionSpec as P

X_PLUS = [(t, (t + 2) % 8) for t in range(8)]
X_MINUS = [(t, (t - 2) % 8) for t in range(8)]
Z_LO = [(t, t ^ 1) for t in range(8)]
Y_PLUS = [(s, (s + 4) % 16) for s in range(16)]
Y_MINUS = [(s, (s - 4) % 16) for s in range(16)]
Z_HI = [(s, s ^ 2) for s in range(16)]
CORE = [(s, s ^ 1) for s in range(16)]

F32, BF16, F16 = jnp.float32, jnp.bfloat16, jnp.float16
RES_SCALE = 8.0
GS_SCALE = 2.0 ** -8


def reorder(rows, order):
    blocks = rows.reshape(8, rows.shape[0] // 8, rows.shape[1])
    return jnp.concatenate(
        [lax.dynamic_index_in_dim(blocks, i, 0, keepdims=False) for i in order], 0
    )


def gather_y(shard):
    half = shard.shape[0] // 2
    low = lax.ppermute(shard, "seq", Y_PLUS)
    high = lax.ppermute(shard, "seq", Y_MINUS)
    far_a = lax.ppermute(low[:half], "seq", Y_PLUS)
    far_b = lax.ppermute(high[half:], "seq", Y_MINUS)
    far = jnp.concatenate([far_a, far_b], 0)
    return [shard, high, far, low]


def reduce_x(part):
    u = lax.ppermute(part[2, 0], "tensor", X_PLUS)
    v = lax.ppermute(part[2, 1], "tensor", X_MINUS)
    to_high = jnp.stack([add16(part[1, 0], u), part[1, 1]])
    to_low = jnp.stack([part[3, 0], add16(part[3, 1], v)])
    a = lax.ppermute(to_high, "tensor", X_PLUS)
    b = lax.ppermute(to_low, "tensor", X_MINUS)
    return part[0].astype(F32) + a.astype(F32) + b.astype(F32)


def add16(a, b):
    return (a.astype(F32) + b.astype(F32)).astype(F16)


def reduce_tensor(part):
    total = reduce_x(part)
    other = lax.ppermute(total[1].astype(F16), "tensor", Z_LO)
    return ((total[0] + other.astype(F32)) * (1 / RES_SCALE)).astype(BF16)


def gather_tensor(res):
    pair = jnp.stack([res, lax.ppermute(res, "tensor", Z_LO)])
    low = lax.ppermute(pair, "tensor", X_PLUS)
    high = lax.ppermute(pair, "tensor", X_MINUS)
    far_a = lax.ppermute(low[0], "tensor", X_PLUS)
    far_b = lax.ppermute(high[1], "tensor", X_MINUS)
    return jnp.concatenate([pair, high, far_a[None], far_b[None], low], 0)


def reduce_y(part):
    other = lax.ppermute(part[:, 1], "seq", CORE)
    both = add16(part[:, 0], other)
    half = 4
    u = lax.ppermute(both[:half, 2], "seq", Y_PLUS)
    v = lax.ppermute(both[half:, 2], "seq", Y_MINUS)
    to_high = jnp.concatenate([add16(both[:half, 1], u), both[half:, 1]], 0)
    to_low = jnp.concatenate([both[:half, 3], add16(both[half:, 3], v)], 0)
    a = lax.ppermute(to_high, "seq", Y_PLUS)
    b = lax.ppermute(to_low, "seq", Y_MINUS)
    return both[:, 0].astype(F32) + a.astype(F32) + b.astype(F32)


def per_device(context, out_proj, student, student_map):
    heads = context.shape[1]
    rows = context.shape[0]
    total_rows = rows * 16
    columns = out_proj.shape[1]
    own = lax.axis_index("tensor")
    x, z = own // 2, own % 2
    forward = [((x + i) % 4) * 2 + (z ^ j) for i in range(4) for j in range(2)]
    inverse = [((i - x) % 4) * 2 + (z ^ j) for i in range(4) for j in range(2)]
    acts = reorder(jnp.concatenate([context, student], 1), forward)
    weights = jnp.concatenate([out_proj * -RES_SCALE, student_map * RES_SCALE], 0)
    weights = weights.astype(BF16)
    acts_z = lax.ppermute(acts, "seq", Z_HI)

    grad_map = None
    grads = []
    for source in (acts, acts_z):
        pieces = jnp.stack(gather_y(source))
        other = lax.ppermute(pieces, "seq", CORE)
        full = jnp.stack([pieces, other]).reshape(8, 8, rows // 8, acts.shape[1])
        full = full.transpose(1, 0, 2, 3).reshape(8 * rows, acts.shape[1])
        part = jnp.dot(full, weights, preferred_element_type=F32).astype(F16)
        res = reduce_tensor(part.reshape(4, 2, rows, columns))
        res = gather_tensor(res).reshape(8 * rows, columns)
        grad = lax.dot_general(
            res, student_map, (((1,), (1,)), ((), ())), preferred_element_type=F32
        )
        grad = (grad * GS_SCALE).astype(F16)
        grads.append(reduce_y(grad.reshape(8, 2, 4, rows // 8, student.shape[1])))
        gm = lax.dot_general(
            full[:, heads:], res, (((0,), (0,)), ((), ())), preferred_element_type=F32
        )
        grad_map = gm if grad_map is None else grad_map + gm
    grad_map = grad_map / total_rows
    far = lax.ppermute(grads[1].astype(F16), "seq", Z_HI)
    grad_student = (grads[0] + far.astype(F32)) * (1 / GS_SCALE)
    grad_student = grad_student.reshape(rows, student.shape[1])
    grad_student = reorder(grad_student, inverse)
    return (grad_map, grad_student)


def solution(mesh):
    return jax.shard_map(
        per_device,
        mesh=mesh,
        in_specs=(P("seq", "tensor"), P("tensor", "seq"), P("seq", "tensor"), P("tensor", "seq")),
        out_specs=(P("tensor", "seq"), P("seq", "tensor")),
        check_vma=False,
    )
```

```python
import jax
import jax.numpy as jnp
from jax import lax
from jax.sharding import PartitionSpec as P


def along_tensor(step):
    return [(t, (t + 2 * step) % 8) for t in range(8)]


def along_y(step, flip=0):
    return [(s, ((s + 4 * step) % 16) ^ flip) for s in range(16)]


X_PLUS, X_MINUS = along_tensor(1), along_tensor(-1)
Y_PLUS, Y_MINUS, Y_TWO = along_y(1), along_y(-1), along_y(2)
Z_LO = [(t, t ^ 1) for t in range(8)]
Z_HI = [(s, s ^ 2) for s in range(16)]
CORE = [(s, s ^ 1) for s in range(16)]
Y_SPLIT = [(s, (s + (4 if s % 2 == 0 else -4)) % 16) for s in range(16)]
X_SPLIT = [
    (t * 16 + s, ((t + (2 if s % 2 == 0 else -2)) % 8) * 16 + s)
    for t in range(8)
    for s in range(16)
]

F32, BF16, F16 = jnp.float32, jnp.bfloat16, jnp.float16
RES_SCALE = 8.0
GS_SCALE = 2.0 ** -8


def seq(value, pairs):
    return lax.ppermute(value, "seq", pairs)


def tensor(value, pairs):
    return lax.ppermute(value, "tensor", pairs)


def add16(a, b):
    return (a.astype(F32) + b.astype(F32)).astype(F16)


class Order:
    def __init__(self, token):
        self.token = token

    def __call__(self, *values):
        *values, self.token = lax.optimization_barrier((*values, self.token))
        return values[0] if len(values) == 1 else values


def rotate(rows, shift, swap):
    blocks = rows.reshape(4, 2, rows.shape[0] // 8, rows.shape[1])
    blocks = jnp.where(swap == 1, blocks[:, ::-1], blocks)
    blocks = jnp.concatenate([blocks, blocks], 0)
    return lax.dynamic_slice_in_dim(blocks, shift, 4, 0).reshape(rows.shape)


def together(shards):
    width = shards[0].shape[-1]
    blocks = [s.reshape(8, -1, width) for s in shards]
    return jnp.concatenate(blocks, 1).reshape(-1, width)


def per_device(context, out_proj, student, student_map):
    heads = context.shape[1]
    rows = context.shape[0]
    total_rows = rows * 16
    columns = out_proj.shape[1]
    width = student.shape[1]
    own = lax.axis_index("tensor")
    first = lax.axis_index("seq") % 2 == 0
    x, z = own // 2, own % 2
    acts = rotate(jnp.concatenate([context, student], 1), x, z)
    step = Order(jnp.zeros((8, 128), F32))
    acts = step(acts)

    def project(full):
        part = jnp.dot(full[:, heads:], student_map, preferred_element_type=F32)
        part -= jnp.dot(full[:, :heads], out_proj, preferred_element_type=F32)
        return (part * RES_SCALE).astype(F16).reshape(4, 2, -1, columns)

    def send_far(part):
        return lax.ppermute(part[2], ("tensor", "seq"), X_SPLIT)

    def send_near(part, u):
        to_high = jnp.where(first, add16(part[1], u), part[1])
        to_low = jnp.where(first, part[3], add16(part[3], u))
        to_high, to_low = step(to_high, to_low)
        return tensor(to_high, X_PLUS), tensor(to_low, X_MINUS)

    def send_z(own, a, b):
        total = (own.astype(F32) + a.astype(F32) + b.astype(F32)).astype(F16)
        total = step(total)
        return total, tensor(total, Z_LO)

    def residual(total, other):
        total = total.astype(F32) + other[::-1].astype(F32)
        res = step((total * (1 / RES_SCALE)).astype(BF16))
        return res, tensor(res, X_PLUS), tensor(res, X_MINUS)

    def pass_on(low, high):
        near = step(jnp.where(first, low, high))
        return lax.ppermute(near, ("tensor", "seq"), X_SPLIT)

    def student_grad(res, count):
        grad = lax.dot_general(
            res, student_map, (((1,), (1,)), ((), ())), preferred_element_type=F32
        )
        grad = (grad * GS_SCALE).astype(F16).reshape(8, 2, count, rows // 8, width)
        grad = step(grad)
        return grad, seq(grad[:, 1], CORE)

    def send_home(grad, other, homes):
        both = step(add16(grad[:, 0], other))
        return [both[:, j] if h is None else seq(both[:, j], h) for j, h in enumerate(homes)]

    def map_grad(full, res):
        return lax.dot_general(
            full[:, heads:], res, (((0,), (0,)), ((), ())), preferred_element_type=F32
        )

    homes = [
        [None, Y_PLUS, Y_MINUS],
        [Z_HI, Y_TWO],
        [along_y(1, 2), along_y(-1, 2), along_y(2, 2)],
    ]
    low, high, zact = seq(acts, Y_PLUS), seq(acts, Y_MINUS), seq(acts, Z_HI)
    other = seq(acts, CORE)
    low, high, other = step(low, high, other)
    near = step(jnp.where(first, low, high))
    far = seq(near, Y_SPLIT)
    other_high, other_low = seq(high, CORE), seq(low, CORE)
    zact = step(zact)
    zlow, zhigh = seq(zact, Y_PLUS), seq(zact, Y_MINUS)
    other_zact = seq(zact, CORE)
    other_high, other_low = step(other_high, other_low)
    full0 = step(together([acts, high, low, other, other_high, other_low]))
    part0 = step(project(full0))
    u0 = send_far(part0)
    far = step(far)
    zfar = seq(far, Z_HI)
    other_far = seq(far, CORE)
    other_far, other_zact = step(other_far, other_zact)
    full1 = step(together([zact, far, other_zact, other_far]))
    part1 = step(project(full1))
    u1 = send_far(part1)
    u0 = step(u0)
    a0, b0 = send_near(part0, u0)
    u1 = step(u1)
    a1, b1 = send_near(part1, u1)
    zlow, zhigh = step(zlow, zhigh)
    other_zlow, other_zhigh = seq(zlow, CORE), seq(zhigh, CORE)
    a0, b0 = step(a0, b0)
    t0, o0 = send_z(part0[0], a0, b0)
    zfar = step(zfar)
    other_zfar = seq(zfar, CORE)
    other_zfar, other_zlow, other_zhigh = step(other_zfar, other_zlow, other_zhigh)
    full2 = step(together([zhigh, zlow, zfar, other_zhigh, other_zlow, other_zfar]))
    part2 = step(project(full2))
    u2 = send_far(part2)
    a1, b1 = step(a1, b1)
    t1, o1 = send_z(part1[0], a1, b1)
    o0 = step(o0)
    res0, low0, high0 = residual(t0, o0)
    u2 = step(u2)
    a2, b2 = send_near(part2, u2)
    o1 = step(o1)
    res1, low1, high1 = residual(t1, o1)
    low0, high0 = step(low0, high0)
    far0 = pass_on(low0, high0)
    a2, b2 = step(a2, b2)
    t2, o2 = send_z(part2[0], a2, b2)
    low1, high1 = step(low1, high1)
    far1 = pass_on(low1, high1)
    far0 = step(far0)
    all0 = jnp.stack([res0, high0, far0, low0]).reshape(-1, columns)
    grad0, c0 = student_grad(all0, 3)
    o2 = step(o2)
    res2, low2, high2 = residual(t2, o2)
    c0 = step(c0)
    home0 = send_home(grad0, c0, homes[0])
    gm = step(map_grad(full0, all0))
    far1 = step(far1)
    all1 = jnp.stack([res1, high1, far1, low1]).reshape(-1, columns)
    grad1, c1 = student_grad(all1, 2)
    low2, high2 = step(low2, high2)
    far2 = pass_on(low2, high2)
    c1 = step(c1)
    home1 = send_home(grad1, c1, homes[1])
    gm = step(gm + map_grad(full1, all1))
    far2 = step(far2)
    all2 = jnp.stack([res2, high2, far2, low2]).reshape(-1, columns)
    grad2, c2 = student_grad(all2, 3)
    c2 = step(c2)
    home2 = send_home(grad2, c2, homes[2])
    gm = (gm + map_grad(full2, all2)) / total_rows
    gm = step(gm)
    grad_student = sum(v.astype(F32) for v in home0 + home1 + home2)
    grad_student = grad_student.reshape(rows, width) * (1 / GS_SCALE)
    return (gm, rotate(grad_student, (4 - x) % 4, z))


def solution(mesh):
    return jax.shard_map(
        per_device,
        mesh=mesh,
        in_specs=(P("seq", "tensor"), P("tensor", "seq"), P("seq", "tensor"), P("tensor", "seq")),
        out_specs=(P("tensor", "seq"), P("seq", "tensor")),
        check_vma=False,
    )
```

```python
import jax
import jax.numpy as jnp
from jax import lax
from jax.sharding import PartitionSpec as P


def along_tensor(step):
    return [(t, (t + 2 * step) % 8) for t in range(8)]


def along_y(step, flip=0):
    return [(s, ((s + 4 * step) % 16) ^ flip) for s in range(16)]


def split_y(step, flip=0):
    return [(s, ((s + (4 if s % 2 == 0 else -4) * step) % 16) ^ flip) for s in range(16)]


X_PLUS, X_MINUS = along_tensor(1), along_tensor(-1)
Y_TWO = along_y(2)
Z_LO = [(t, t ^ 1) for t in range(8)]
Z_HI = [(s, s ^ 2) for s in range(16)]
CORE = [(s, s ^ 1) for s in range(16)]
Y_SPLIT = split_y(1)
X_SPLIT = [
    (t * 16 + s, ((t + (2 if s % 2 == 0 else -2)) % 8) * 16 + s)
    for t in range(8)
    for s in range(16)
]

F32, BF16, F16 = jnp.float32, jnp.bfloat16, jnp.float16
RES_SCALE = 8.0
GS_SCALE = 2.0 ** -8


def seq(value, pairs):
    return lax.ppermute(value, "seq", pairs)


def tensor(value, pairs):
    return lax.ppermute(value, "tensor", pairs)


def add16(a, b):
    return (a.astype(F32) + b.astype(F32)).astype(F16)


def zero_of(value):
    corner = lax.slice(value, (0,) * value.ndim, (1,) * value.ndim)
    return corner.reshape(()).astype(F32) * 0.0


def tied(value, deps):
    for v in deps:
        value = (value.astype(F32) + zero_of(v)).astype(value.dtype)
    return value


LANES = 128


class Order:
    def __init__(self, token):
        self.token = token

    def __call__(self, *values):
        *values, self.token = lax.optimization_barrier((*values, self.token))
        return values[0] if len(values) == 1 else values


def rotate(rows, shift, swap):
    blocks = rows.reshape(4, 2, rows.shape[0] // 8, rows.shape[1])
    blocks = jnp.where(swap == 1, blocks[:, ::-1], blocks)
    blocks = jnp.concatenate([blocks, blocks], 0)
    return lax.dynamic_slice_in_dim(blocks, shift, 4, 0).reshape(rows.shape)


def together(shards):
    width = shards[0].shape[-1]
    blocks = [s.reshape(8, -1, width) for s in shards]
    return jnp.concatenate(blocks, 1).reshape(-1, width)


def per_device(context, out_proj, student, student_map):
    heads = context.shape[1]
    rows = context.shape[0]
    total_rows = rows * 16
    columns = out_proj.shape[1]
    width = student.shape[1]
    own = lax.axis_index("tensor")
    first = lax.axis_index("seq") % 2 == 0
    x, z = own // 2, own % 2
    acts = rotate(jnp.concatenate([context, student], 1), x, z)
    step = Order(jnp.zeros((8, 128), F32))
    acts = step(acts)

    def project(full):
        part = jnp.dot(full[:, heads:], student_map, preferred_element_type=F32)
        part -= jnp.dot(full[:, :heads], out_proj, preferred_element_type=F32)
        return (part * RES_SCALE).astype(F16).reshape(4, 2, -1, columns)

    def all_rows(pieces):
        return together([p[j : j + rows] for p in pieces for j in range(0, p.shape[0], rows)])

    def send_far(part):
        return lax.ppermute(part[2].astype(F16), ("tensor", "seq"), X_SPLIT)

    def send_near(part, u, *deps):
        u = u.astype(F32)
        to_high = tied(jnp.where(first, part[1] + u, part[1]), deps).astype(F16)
        to_low = tied(jnp.where(first, part[3], part[3] + u), deps).astype(F16)
        return tensor(to_high, X_PLUS), tensor(to_low, X_MINUS)

    def send_z(own, a, b, *deps):
        total = tied(own + a.astype(F32) + b.astype(F32), deps).astype(F16)
        total = step(total)
        return total, tensor(total, Z_LO)

    def residual(total, other, *deps):
        total = total.astype(F32) + other[::-1].astype(F32)
        res = step(tied(total * (1 / RES_SCALE), deps).astype(BF16))
        return res, tensor(res, X_PLUS), tensor(res, X_MINUS)

    def pass_on(low, high, *deps):
        near = step(tied(jnp.where(first, low, high), deps))
        return lax.ppermute(near, ("tensor", "seq"), X_SPLIT)

    def student_grad(res, keep, give, *deps):
        grad = lax.dot_general(
            res, student_map, (((1,), (1,)), ((), ())), preferred_element_type=F32
        )
        grad = tied(grad * GS_SCALE, deps).astype(F16).reshape(8, -1, rows // 8, width)
        grad = step(grad)
        give = jnp.stack([grad[:, j] for j in give])
        return [grad[:, j] for j in keep], seq(give, CORE)

    def send_home(kept, given, homes, *deps):
        both = [tied(add16(k, given[j]), deps) for j, k in enumerate(kept)]
        both = step(*both)
        return [v if h is None else seq(v, h) for v, h in zip(both, homes)]

    def map_grad(full, res):
        return lax.dot_general(
            full[:, heads:], res, (((0,), (0,)), ((), ())), preferred_element_type=F32
        )

    def pair_of(shard, other):
        return jnp.concatenate([shard, other], 0)

    zact = seq(acts, Z_HI)
    pair = step(pair_of(acts, seq(acts, CORE)))
    recv = seq(pair, Y_SPLIT)
    recv = step(recv)
    far = seq(recv[:rows], Y_SPLIT)
    zact = step(zact)
    zpair = step((pair_of(zact, seq(zact, CORE)).astype(F32) + recv[:1].astype(F32) * 0.0).astype(BF16))
    zrecv = seq(zpair, Y_SPLIT)
    swap = step(seq(recv, CORE))
    shards0 = step(pair, recv, swap, zpair)
    full0 = step(all_rows(shards0))
    part0 = step(project(full0))
    u0 = send_far(part0)
    other_far = seq(far, CORE)
    zfar = seq(zrecv[:rows], Y_SPLIT)
    zswap = seq(zrecv, CORE)
    a0, b0 = send_near(part0, u0)
    other_zfar = seq(zfar, CORE)
    t0, o0 = send_z(part0[0], a0, b0)
    shards1 = zrecv, zswap, far, other_far, zfar, other_zfar
    full1 = step(all_rows(shards1))
    part1 = step(project(full1))
    u1 = send_far(part1)
    a1, b1 = send_near(part1, u1)
    res0, low0, high0 = residual(t0, o0)
    far0 = pass_on(low0, high0)
    t1, o1 = send_z(part1[0], a1, b1)
    res1, low1, high1 = residual(t1, o1)
    all0 = jnp.stack([res0, high0, far0, low0]).reshape(-1, columns)
    grad0, c0 = student_grad(all0, (0, 5, 2, 6), (1, 3, 4, 7))
    home0 = send_home(grad0, c0, [None, Y_SPLIT, split_y(-1), Z_HI])
    far1 = pass_on(low1, high1, *home0[1:])
    gm = map_grad(full0, all0)
    all1 = jnp.stack([res1, high1, far1, low1]).reshape(-1, columns)
    grad1, c1 = student_grad(all1, (3, 0, 4, 6), (1, 2, 5, 7), gm)
    home1 = send_home(
        grad1, c1, [split_y(1, 2), split_y(-1, 2), Y_TWO, along_y(2, 2)]
    )
    gm = (gm + map_grad(full1, all1)) / total_rows
    gm = step(gm)
    early = sum(v.astype(F32) for v in home0)
    grad_student = early + sum(v.astype(F32) for v in home1)
    grad_student = grad_student.reshape(rows, width) * (1 / GS_SCALE)
    return (gm, rotate(grad_student, (4 - x) % 4, z))


def solution(mesh):
    return jax.shard_map(
        per_device,
        mesh=mesh,
        in_specs=(P("seq", "tensor"), P("tensor", "seq"), P("seq", "tensor"), P("tensor", "seq")),
        out_specs=(P("tensor", "seq"), P("seq", "tensor")),
        check_vma=False,
    )
```
